256 devices in a mesh: tok: 16 (over y, x_hi, core), feat: 16 (over z, x_lo).
Axes of the slice: x: 4 (x_hi: 2, x_lo: 2; x = x_hi * 2 + x_lo), y: 4, z: 8, core: 2. Of those that a mesh axis runs over, the one named last changes fastest.
Arguments:
- gradients: bfloat16 [8192, 6912], P('tok', 'feat'), may hold values from -30 to 30
- previous: float32 [6912, 6912], P(('feat', 'tok')), may hold values from -4 to 4
Outputs:
- factor: float32 [6912, 6912], P(('feat', 'tok'))
The draws below stay inside these ranges and needn't reach their ends.
All inputs are finite; a program needn't handle non-finite values.
Results may differ from the reference program's by a relative error of at most 0.0003.
Values may be sent and summed in bfloat16 or wider, within the bound.
No kernel may reach another device: no remote copies, remote signals or barrier semaphores. Data moves between devices by JAX's collectives and lax.ppermute only.
A program may use at most 64 MiB of HBM per device.

```python
import math
import jax
import jax.numpy as jnp
from jax import lax

FW = 6912
PRIOR = 1
TOKENS = 8192


def draw_gradients(key, part):
    key = jax.random.fold_in(key, 11)
    keys = jax.random.split(key, 5)
    tok_scale = jnp.exp(jax.random.uniform(keys[0], (TOKENS, 1), jnp.float32, math.log(0.3), math.log(3.0)))
    feat_scale = jnp.exp(jax.random.uniform(keys[1], (1, FW), jnp.float32, math.log(0.5), math.log(2.0)))
    base = jnp.clip(jax.random.normal(keys[2], (TOKENS, FW), jnp.float32), -4.0, 4.0)
    common = 0.3
    shared = jax.random.normal(keys[3], (TOKENS, 1), jnp.float32) * jax.random.normal(keys[4], (1, FW), jnp.float32)
    values = tok_scale * feat_scale * (base + common * shared)
    return jnp.clip(values, -30.0, 30.0).astype(jnp.bfloat16)


def levels(own_key, extent, cuts, smallest, largest):
    loudness, own = 1.0, jax.random.fold_in(own_key, 6)
    for dim, parts in cuts:
        steps = jnp.exp(jax.random.uniform(jax.random.fold_in(own, dim), (parts,), jnp.float32, smallest / len(cuts), largest / len(cuts)))
        loudness = loudness * jnp.repeat(steps, extent[dim] // parts).reshape([-1 if axis == dim else 1 for axis in range(len(extent))])
    return loudness


def bell_draw(stream_key, dims, scale, bound, shards=(), kind=jnp.bfloat16):
    level = levels(stream_key, dims, shards, -0.22, 0.18) if shards else 1.0
    drawn = jax.random.normal(stream_key, dims, jnp.float32) * scale * level
    return jnp.minimum(jnp.maximum(drawn, -bound), bound).astype(kind)


def setup_inputs(seed: int = 0) -> dict:
    key_list = jax.random.split(jax.random.key(seed), 3)
    gradients = draw_gradients(jax.random.fold_in(key_list[2], 71), 0)
    previous = bell_draw(key_list[1], (FW, FW), 0.5, 4.0, ((0, 256),), jnp.float32)
    return {"gradients": gradients, "previous": previous}


def reference(gradients, previous):
    values = gradients.astype(jnp.float32)
    cov_sum = jnp.dot(values.T, values, precision=lax.Precision.HIGHEST, preferred_element_type=jnp.float32)
    return (PRIOR * previous + cov_sum / TOKENS) / (PRIOR + 1)
```

```python
import functools

import jax
import jax.numpy as jnp
from jax import lax
from jax.experimental import pallas as pl
from jax.experimental.pallas import tpu as pltpu
from jax.sharding import PartitionSpec as P

PRIOR = 1
AXES = ("tok", "feat")
NY, NXH, NC, NZ, NXL = 4, 2, 2, 8, 2
N_TOK, N_FEAT = NY * NXH * NC, NZ * NXL


def linear(y, xh, c, z, xl):
    return ((y % NY * NXH + xh % NXH) * NC + c % NC) * N_FEAT + z % NZ * NXL + xl % NXL


def move(value, where):
    pairs = []
    for y in range(NY):
        for xh in range(NXH):
            for c in range(NC):
                for z in range(NZ):
                    for xl in range(NXL):
                        to = where(y, xh, c, z, xl)
                        if to is not None:
                            pairs.append((linear(y, xh, c, z, xl), linear(*to)))
    return lax.ppermute(value, AXES, pairs)


def along_z(value, by):
    return move(value, lambda y, xh, c, z, xl: (y, xh, c, z + by, xl))


def along_y(value, by):
    return move(value, lambda y, xh, c, z, xl: (y + by, xh, c, z, xl))


def other_xl(value):
    return move(value, lambda y, xh, c, z, xl: (y, xh, c, z, xl + 1))


def other_xh(value):
    return move(value, lambda y, xh, c, z, xl: (y, xh + 1, c, z, xl))


def other_core(value):
    return move(value, lambda y, xh, c, z, xl: (y, xh, c + 1, z, xl))


def products_kernel(units, n_shards, width, *refs):
    sources, out = refs[: 2 * n_shards], refs[2 * n_shards]
    held, full, arrived = refs[2 * n_shards + 1 :]
    core = lax.rem(lax.axis_index("tok"), NC)
    n_rows = width // (NY * NXH)
    depth = held.shape[2]
    half = depth // 2
    copies = []
    for i in range(n_shards):
        for side in range(2):
            place = held.at[i, :, side * half : (side + 1) * half]
            copies.append(pltpu.make_async_copy(sources[2 * i + side], place, arrived.at[i, side]))
            copies[-1].start()
    peak = jnp.zeros((16, depth), jnp.float32)
    for i in range(n_shards):
        copies[2 * i].wait()
        copies[2 * i + 1].wait()
        rows = jnp.max(jnp.abs(held[i]).reshape(width // 16, 16, depth), axis=0)
        peak = jnp.maximum(peak, rows.astype(jnp.float32))
    peak = jnp.maximum(jnp.max(peak), 1e-18)

    for c in range(NC):

        @pl.when(core == c)
        def _():
            for slot, (a, b) in enumerate(units[c]):
                full[:width, slot * width : (slot + 1) * width] = lax.dot_general(
                    held[a], held[b], (((1,), (1,)), ((), ())), preferred_element_type=jnp.float32
                )

    column = lax.broadcasted_iota(jnp.int32, (1, full.shape[1]), 1)
    fraction = lax.rem(column * 7, 16).astype(jnp.float32) * 0.0625
    exponent = jnp.ceil(2.0 * jnp.log2(jnp.full((1, full.shape[1]), peak))) + (depth.bit_length() - 15) + fraction
    exponents = jnp.broadcast_to(jnp.maximum(exponent, -125.0), (out.shape[2] - n_rows, full.shape[1]))
    for k in range(NY * NXH):
        out[k // NXH, k % NXH, :n_rows, :] = full[k * n_rows : (k + 1) * n_rows, :]
        out[k // NXH, k % NXH, n_rows:, :] = exponents


def products(units, shards):
    width, half = shards[0][0].shape
    n_units = len(units[0])
    padded = -(-(width // (NY * NXH)) // 8) * 8
    flat = [side for shard in shards for side in shard]
    return pl.pallas_call(
        functools.partial(products_kernel, units, len(shards), width),
        out_shape=jax.ShapeDtypeStruct((NY, NXH, padded, n_units * width), jnp.float32),
        in_specs=[pl.BlockSpec(memory_space=pl.ANY)] * len(flat),
        out_specs=pl.BlockSpec(memory_space=pltpu.VMEM),
        scratch_shapes=[
            pltpu.VMEM((len(shards), width, 2 * half), shards[0][0].dtype),
            pltpu.VMEM((width, n_units * width), jnp.float32),
            pltpu.SemaphoreType.DMA((len(shards), 2)),
        ],
        compiler_params=pltpu.CompilerParams(vmem_limit_bytes=20 * 1024 * 1024),
        cost_estimate=pl.CostEstimate(
            flops=n_units * 4 * width * width * half, bytes_accessed=8 * 1024 * 1024, transcendentals=0
        ),
    )(*flat)


def at_exponent(value, n_rows):
    return lax.broadcasted_iota(jnp.int32, value.shape, value.ndim - 2) == n_rows


def exponent_row(value, n_rows):
    return lax.slice_in_dim(value, n_rows, n_rows + 1, axis=value.ndim - 2)


def packed(value, n_rows):
    scaled = value * jnp.exp2(-exponent_row(value, n_rows))
    return jnp.where(at_exponent(value, n_rows), value, scaled).astype(jnp.float16)


def unpacked(value, n_rows):
    value = value.astype(jnp.float32)
    return jnp.where(at_exponent(value, n_rows), value, value * jnp.exp2(exponent_row(value, n_rows)))


def added(a, b, n_rows):
    return jnp.where(at_exponent(a, n_rows), jnp.maximum(a, b) + 1.3125, a + b)


def tied(value, *others):
    return lax.optimization_barrier((value, *others))[0]


def chunk_of(part, at):
    return lax.dynamic_index_in_dim(part, lax.rem(at, part.shape[0]), 0, keepdims=False)


def y_first(part, n_rows, y_at):
    far = chunk_of(part, y_at + 2)
    return along_y(packed(far[0], n_rows), 1), along_y(packed(far[1], n_rows), -1)


def y_second(part, arrived, n_rows, y_at):
    above, below = chunk_of(part, y_at + 1), chunk_of(part, y_at + 3)
    first = added(above[0], unpacked(arrived[0], n_rows), n_rows)
    second = added(below[1], unpacked(arrived[1], n_rows), n_rows)
    to_above = packed(jnp.stack([first, above[1]]), n_rows)
    to_below = packed(jnp.stack([below[0], second]), n_rows)
    return to_above, to_below


def y_last(part, arrived, n_rows, y_at):
    summed = added(unpacked(arrived[0], n_rows), unpacked(arrived[1], n_rows), n_rows)
    return added(chunk_of(part, y_at), summed, n_rows)


def x_give(summed, n_rows, xh_at):
    return packed(chunk_of(summed, xh_at + 1), n_rows)


def x_last(summed, arrived, n_rows, xh_at):
    return chunk_of(summed, xh_at) + unpacked(arrived, n_rows)


HELD = (
    ((1, 0), (-1, 1), (1, 1), (3, 0), (4, 0), (2, 1), (3, 1), (4, 1)),
    ((2, 0), (-1, 0), (-2, 0), (-3, 0), (0, 1), (0, 0), (-2, 1), (-3, 1)),
)


def assemble_kernel(width, count, mine, theirs, previous, out, stack):
    n_rows = previous.shape[0]
    core = lax.rem(lax.axis_index("tok"), NC)
    feat = lax.axis_index("feat")
    z_at, xl_at = feat // NXL, lax.rem(feat, NXL)
    for c in range(NC):

        @pl.when(core == c)
        def _():
            for slot in range(len(HELD[c])):
                columns = slice(slot * width, (slot + 1) * width)
                dz, dx = HELD[c][slot]
                stack[dz % NZ * NXL + dx, :n_rows, :] = mine[c * n_rows : (c + 1) * n_rows, columns]
                dz, dx = HELD[1 - c][slot]
                stack[dz % NZ * NXL + dx, :n_rows, :] = theirs[:, columns]

    for f in range(N_FEAT):
        at = lax.rem(f // NXL - z_at + NZ, NZ) * NXL + lax.rem(f % NXL + xl_at, NXL)
        columns = slice(f * width, (f + 1) * width)
        cov = stack[at, :n_rows, :] * (1.0 / count)
        out[:, columns] = (PRIOR * previous[:, columns] + cov) * (1.0 / (PRIOR + 1))


def assemble(mine, theirs, previous, width, count):
    n_rows = previous.shape[0]
    return pl.pallas_call(
        functools.partial(assemble_kernel, width, count),
        out_shape=jax.ShapeDtypeStruct(previous.shape, jnp.float32),
        in_specs=[pl.BlockSpec(memory_space=pltpu.VMEM)] * 3,
        out_specs=pl.BlockSpec(memory_space=pltpu.VMEM),
        scratch_shapes=[pltpu.VMEM((N_FEAT, -(-n_rows // 8) * 8, width), jnp.float32)],
        compiler_params=pltpu.CompilerParams(vmem_limit_bytes=14 * 1024 * 1024),
        cost_estimate=pl.CostEstimate(flops=0, bytes_accessed=4 * 1024 * 1024, transcendentals=0),
    )(mine, theirs, previous)


def per_device(gradients, previous):
    width = gradients.shape[1]
    count = gradients.shape[0] * N_TOK
    n_rows = previous.shape[0]
    tok = lax.axis_index("tok")
    y_at, xh_at, c_at = tok // (NXH * NC), lax.rem(tok // NC, NXH), lax.rem(tok, NC)

    own = gradients.T
    after, before, across = along_z(own, -1), along_z(own, 1), other_xl(own)
    own_2 = other_core(own)
    after2, before2 = along_z(after, -1), along_z(before, 1)
    across2 = other_xl(after2)
    after_2, before_2, across_2 = other_core(after), other_core(before), other_core(across)
    after2_2, before2_2 = other_core(after2), other_core(before2)

    near = [
        (own, own_2), (after, after_2), (before, before_2), (across, across_2), (after2, after2_2), (before2, before2_2)
    ]
    rows = n_rows * NC
    part1 = products(
        (((0, 1), (3, 2), (2, 3), (2, 4), (5, 4)), ((0, 4), (1, 0), (4, 0), (4, 2), (0, 3))), near
    )
    half1 = y_first(part1, rows, y_at)
    half1 = (tied(half1[0], across2), half1[1])
    give1 = y_second(part1, half1, rows, y_at)
    got1 = along_y(give1[0], 1), along_y(give1[1], -1)

    across2_2 = other_core(across2)
    far = [(own, own_2), (before, before_2), (before2, before2_2), (across2, across2_2)]
    part2 = products((((0, 3), (1, 3), (2, 3)), ((0, 0), (3, 0), (3, 1))), far)
    half2 = y_first(part2, rows, y_at)
    summed1 = y_last(part1, got1, rows, y_at)
    x_got1 = other_xh(x_give(summed1, rows, xh_at))
    give2 = y_second(part2, half2, rows, y_at)
    got2 = along_y(give2[0], 1), along_y(give2[1], -1)
    sum1 = x_last(summed1, tied(x_got1, give2[0]), rows, xh_at)

    def shifted(value, low, high):
        def where(y, xh, c, z, xl):
            by = (low, high)[c]
            return None if by is None else (y, xh, c, z + by[0], xl + by[1])

        return move(value, where)

    w = width
    got_a = shifted(sum1[:, w : 2 * w], (0, 1), (1, 0))
    got_b = shifted(sum1[:, 2 * w : 4 * w], (-1, 0), (2, 0))
    got_c = jnp.where(c_at == 0, shifted(sum1[:, 4 * w :], (-2, 0), None), sum1[:, 4 * w :])

    summed2 = y_last(part2, got2, rows, y_at)
    x_got2 = other_xh(x_give(summed2, rows, xh_at))
    sum2 = x_last(summed2, tied(x_got2, got_a, got_b, got_c), rows, xh_at)
    got_d = shifted(sum2[:, w : 2 * w], (-1, 0), (2, 1))
    got_e = shifted(sum2[:, 2 * w :], (-2, 0), (2, 1))
    mine = jnp.concatenate([sum1[:, :w], got_a, got_b, got_c, sum2[:, :w], got_d, got_e], axis=1)
    theirs = other_core(lax.dynamic_slice_in_dim(mine, (1 - c_at) * n_rows, n_rows, 0))
    return assemble(mine, theirs, previous, width, count)


def solution(mesh):
    placed = (P("tok", "feat"), P(("feat", "tok"), None))
    return jax.shard_map(
        per_device, mesh=mesh, in_specs=placed, out_specs=P(("feat", "tok"), None), check_vma=False
    )
```

```python
import functools

import jax
import jax.numpy as jnp
from jax import lax
from jax.experimental import pallas as pl
from jax.experimental.pallas import tpu as pltpu
from jax.sharding import PartitionSpec as P

PRIOR = 1
AXES = ("tok", "feat")
NY, NXH, NC, NZ, NXL = 4, 2, 2, 8, 2
N_TOK, N_FEAT = NY * NXH * NC, NZ * NXL


def linear(y, xh, c, z, xl):
    return ((y % NY * NXH + xh % NXH) * NC + c % NC) * N_FEAT + z % NZ * NXL + xl % NXL


def move(value, where, turned=False):
    pairs = []
    for y in range(NY):
        for xh in range(NXH):
            for c in range(NC):
                for z in range(NZ):
                    for xl in range(NXL):
                        to = where(y, xh, c, z, xl)
                        if to is not None:
                            pairs.append((linear(y, xh, c, z, xl), linear(*to)))
    return lax.ppermute(value, AXES, pairs[::-1] if turned else pairs)


def along_z(value, by):
    return move(value, lambda y, xh, c, z, xl: (y, xh, c, z + by, xl))


def along_y(value, by, turned=False):
    return move(value, lambda y, xh, c, z, xl: (y + by, xh, c, z, xl), turned)


def other_xl(value):
    return move(value, lambda y, xh, c, z, xl: (y, xh, c, z, xl + 1))


def other_xh(value):
    return move(value, lambda y, xh, c, z, xl: (y, xh + 1, c, z, xl))


def other_core(value):
    return move(value, lambda y, xh, c, z, xl: (y, xh, c + 1, z, xl))


def products_kernel(units, n_shards, width, *refs):
    sources, out = refs[: 2 * n_shards], refs[2 * n_shards]
    held, full, arrived = refs[2 * n_shards + 1 :]
    core = lax.rem(lax.axis_index("tok"), NC)
    n_rows = width // (NY * NXH)
    depth = held.shape[2]
    half = depth // 2
    copies = []
    for i in range(n_shards):
        for side in range(2):
            place = held.at[i, :, side * half : (side + 1) * half]
            copies.append(pltpu.make_async_copy(sources[2 * i + side], place, arrived.at[i, side]))
            copies[-1].start()
    peak = jnp.zeros((16, depth), jnp.float32)
    for i in range(n_shards):
        copies[2 * i].wait()
        copies[2 * i + 1].wait()
        rows = jnp.max(jnp.abs(held[i]).reshape(width // 16, 16, depth), axis=0)
        peak = jnp.maximum(peak, rows.astype(jnp.float32))
    peak = jnp.maximum(jnp.max(peak), 1e-18)

    for c in range(NC):

        @pl.when(core == c)
        def _():
            for slot, (a, b) in enumerate(units[c]):
                full[:width, slot * width : (slot + 1) * width] = lax.dot_general(
                    held[a], held[b], (((1,), (1,)), ((), ())), preferred_element_type=jnp.float32
                )

    column = lax.broadcasted_iota(jnp.int32, (1, full.shape[1]), 1)
    fraction = lax.rem(column * 7, 16).astype(jnp.float32) * 0.0625
    exponent = jnp.ceil(2.0 * jnp.log2(jnp.full((1, full.shape[1]), peak))) + (depth.bit_length() - 15) + fraction
    exponents = jnp.broadcast_to(jnp.maximum(exponent, -125.0), (out.shape[2] - n_rows, full.shape[1]))
    for k in range(NY * NXH):
        out[k // NXH, k % NXH, :n_rows, :] = full[k * n_rows : (k + 1) * n_rows, :]
        out[k // NXH, k % NXH, n_rows:, :] = exponents


def products(units, shards):
    width, half = shards[0][0].shape
    n_units = len(units[0])
    padded = -(-(width // (NY * NXH)) // 8) * 8
    flat = [side for shard in shards for side in shard]
    return pl.pallas_call(
        functools.partial(products_kernel, units, len(shards), width),
        out_shape=jax.ShapeDtypeStruct((NY, NXH, padded, n_units * width), jnp.float32),
        in_specs=[pl.BlockSpec(memory_space=pl.ANY)] * len(flat),
        out_specs=pl.BlockSpec(memory_space=pltpu.VMEM),
        scratch_shapes=[
            pltpu.VMEM((len(shards), width, 2 * half), shards[0][0].dtype),
            pltpu.VMEM((width, n_units * width), jnp.float32),
            pltpu.SemaphoreType.DMA((len(shards), 2)),
        ],
        compiler_params=pltpu.CompilerParams(vmem_limit_bytes=20 * 1024 * 1024),
        cost_estimate=pl.CostEstimate(
            flops=n_units * 4 * width * width * half, bytes_accessed=8 * 1024 * 1024, transcendentals=0
        ),
    )(*flat)


def at_exponent(value, n_rows):
    return lax.broadcasted_iota(jnp.int32, value.shape, value.ndim - 2) == n_rows


def exponent_row(value, n_rows):
    return lax.slice_in_dim(value, n_rows, n_rows + 1, axis=value.ndim - 2)


def packed(value, n_rows):
    scaled = value * jnp.exp2(-exponent_row(value, n_rows))
    return jnp.where(at_exponent(value, n_rows), value, scaled).astype(jnp.float16)


def unpacked(value, n_rows):
    value = value.astype(jnp.float32)
    return jnp.where(at_exponent(value, n_rows), value, value * jnp.exp2(exponent_row(value, n_rows)))


def added(a, b, n_rows):
    return jnp.where(at_exponent(a, n_rows), jnp.maximum(a, b) + 1.3125, a + b)


def tied(value, *others):
    return lax.optimization_barrier((value, *others))[0]


def chunk_of(part, at):
    return lax.dynamic_index_in_dim(part, lax.rem(at, part.shape[0]), 0, keepdims=False)


def y_first(part, n_rows, y_at):
    far = chunk_of(part, y_at + 2)
    return packed(far[0], n_rows), packed(far[1], n_rows)


def y_second(part, arrived, n_rows, y_at):
    above, below = chunk_of(part, y_at + 1), chunk_of(part, y_at + 3)
    first = added(above[0], unpacked(arrived[0], n_rows), n_rows)
    second = added(below[1], unpacked(arrived[1], n_rows), n_rows)
    to_above = packed(jnp.stack([first, above[1]]), n_rows)
    to_below = packed(jnp.stack([below[0], second]), n_rows)
    return to_above, to_below


def y_last(part, arrived, n_rows, y_at):
    summed = added(unpacked(arrived[0], n_rows), unpacked(arrived[1], n_rows), n_rows)
    return added(chunk_of(part, y_at), summed, n_rows)


def x_give(summed, n_rows, xh_at):
    return packed(chunk_of(summed, xh_at + 1), n_rows)


def x_last(summed, arrived, n_rows, xh_at):
    return chunk_of(summed, xh_at) + unpacked(arrived, n_rows)


HELD = (
    ((1, 0), (-1, 1), (1, 1), (3, 0), (0, 0), (3, 1), (4, 0), (4, 1)),
    ((2, 0), (-1, 0), (-2, 0), (-3, 0), (0, 1), (2, 1), (-2, 1), (-3, 1)),
)


def assemble_kernel(width, count, mine, theirs, previous, out, stack):
    n_rows = previous.shape[0]
    core = lax.rem(lax.axis_index("tok"), NC)
    feat = lax.axis_index("feat")
    z_at, xl_at = feat // NXL, lax.rem(feat, NXL)
    for c in range(NC):

        @pl.when(core == c)
        def _():
            for slot in range(len(HELD[c])):
                columns = slice(slot * width, (slot + 1) * width)
                dz, dx = HELD[c][slot]
                stack[dz % NZ * NXL + dx, :n_rows, :] = mine[c * n_rows : (c + 1) * n_rows, columns]
                dz, dx = HELD[1 - c][slot]
                stack[dz % NZ * NXL + dx, :n_rows, :] = theirs[:, columns]

    for f in range(N_FEAT):
        at = lax.rem(f // NXL - z_at + NZ, NZ) * NXL + lax.rem(f % NXL + xl_at, NXL)
        columns = slice(f * width, (f + 1) * width)
        cov = stack[at, :n_rows, :] * (1.0 / count)
        out[:, columns] = (PRIOR * previous[:, columns] + cov) * (1.0 / (PRIOR + 1))


def assemble(mine, theirs, previous, width, count):
    n_rows = previous.shape[0]
    return pl.pallas_call(
        functools.partial(assemble_kernel, width, count),
        out_shape=jax.ShapeDtypeStruct(previous.shape, jnp.float32),
        in_specs=[pl.BlockSpec(memory_space=pltpu.VMEM)] * 3,
        out_specs=pl.BlockSpec(memory_space=pltpu.VMEM),
        scratch_shapes=[pltpu.VMEM((N_FEAT, -(-n_rows // 8) * 8, width), jnp.float32)],
        compiler_params=pltpu.CompilerParams(vmem_limit_bytes=14 * 1024 * 1024),
        cost_estimate=pl.CostEstimate(flops=0, bytes_accessed=4 * 1024 * 1024, transcendentals=0),
    )(mine, theirs, previous)


def per_device(gradients, previous):
    width = gradients.shape[1]
    count = gradients.shape[0] * N_TOK
    n_rows = previous.shape[0]
    tok = lax.axis_index("tok")
    y_at, xh_at, c_at = tok // (NXH * NC), lax.rem(tok // NC, NXH), lax.rem(tok, NC)

    own = gradients.T
    after, before, across = along_z(own, -1), along_z(own, 1), other_xl(own)
    own_2 = other_core(own)
    after2, before2 = along_z(after, -1), along_z(before, 1)
    across2 = other_xl(after2)
    after_2, before_2, across_2 = (other_core(tied(shard, own_2)) for shard in (after, before, across))
    after2_2 = other_core(after2)

    near = [(own, own_2), (after, after_2), (before, before_2), (across, across_2), (after2, after2_2)]
    rows = n_rows * NC
    part1 = products(
        (((0, 1), (3, 2), (2, 3), (2, 4), (0, 0)), ((0, 4), (1, 0), (4, 0), (4, 2), (0, 3))), near
    )
    far1 = y_first(part1, rows, y_at)
    half1 = along_y(far1[0], 1), along_y(far1[1], -1)
    across2_2, before2_2 = other_core(tied(across2, *far1)), other_core(tied(before2, *far1))

    far = [(own, own_2), (before, before_2), (before2, before2_2), (across2, across2_2), (after2, after2_2)]
    part2 = products((((1, 3), (2, 4), (2, 3)), ((0, 3), (3, 0), (3, 1))), far)
    far2 = y_first(part2, rows, y_at)
    half2 = along_y(far2[0], 1, True), along_y(far2[1], -1, True)
    half1 = lax.optimization_barrier(half1)
    give1 = y_second(part1, half1, rows, y_at)
    got1 = lax.optimization_barrier((along_y(give1[0], 1), along_y(give1[1], -1)))
    half2 = lax.optimization_barrier((*half2, *give1))[:2]
    give2 = y_second(part2, half2, rows, y_at)
    got2 = lax.optimization_barrier((along_y(give2[0], 1, True), along_y(give2[1], -1, True)))
    summed1 = y_last(part1, got1, rows, y_at)
    x_got1 = other_xh(x_give(summed1, rows, xh_at))
    sum1 = x_last(summed1, x_got1, rows, xh_at)

    def shifted(value, low, high, xh_by=0):
        def where(y, xh, c, z, xl):
            by = (low, high)[c]
            return None if by is None else (y, xh + xh_by, c, z + by[0], xl + by[1])

        return move(value, where)

    w = width
    got_a = shifted(sum1[:, w : 2 * w], (0, 1), (1, 0))
    got_b = shifted(sum1[:, 2 * w : 4 * w], (-1, 0), (2, 0))
    summed2 = y_last(part2, got2, rows, y_at)
    keep, give = chunk_of(summed2, xh_at), packed(chunk_of(summed2, xh_at + 1), rows)
    kept = packed(keep, rows)
    d_same, d_other = shifted(kept[:, :w], (-1, 0), None), shifted(give[:, :w], (-1, 0), (0, 0), 1)
    e_same, e_other = shifted(kept[:, w:], (-2, 0), (2, 1)), shifted(give[:, w:], (-2, 0), (2, 1), 1)
    d_same, d_other, e_same, e_other = lax.optimization_barrier((d_same, d_other, e_same, e_other))
    got_d = jnp.where(c_at == 0, unpacked(d_same, rows), keep[:, :w]) + unpacked(d_other, rows)
    got_e = unpacked(e_same, rows) + unpacked(e_other, rows)
    mine = jnp.concatenate([sum1[:, :w], got_a, got_b, sum1[:, 4 * w :], got_d, got_e], axis=1)
    theirs = other_core(lax.dynamic_slice_in_dim(mine, (1 - c_at) * n_rows, n_rows, 0))
    return assemble(mine, theirs, previous, width, count)


def solution(mesh):
    placed = (P("tok", "feat"), P(("feat", "tok"), None))
    return jax.shard_map(
        per_device, mesh=mesh, in_specs=placed, out_specs=P(("feat", "tok"), None), check_vma=False
    )
```

```python
import functools

import jax
import jax.numpy as jnp
from jax import lax
from jax.experimental import pallas as pl
from jax.experimental.pallas import tpu as pltpu
from jax.sharding import PartitionSpec as P

PRIOR = 1
AXES = ("tok", "feat")
NY, NXH, NC, NZ, NXL = 4, 2, 2, 8, 2
N_TOK, N_FEAT = NY * NXH * NC, NZ * NXL


def linear(y, xh, c, z, xl):
    return ((y % NY * NXH + xh % NXH) * NC + c % NC) * N_FEAT + z % NZ * NXL + xl % NXL


def move(value, where, turned=False):
    pairs = []
    for y in range(NY):
        for xh in range(NXH):
            for c in range(NC):
                for z in range(NZ):
                    for xl in range(NXL):
                        to = where(y, xh, c, z, xl)
                        if to is not None:
                            pairs.append((linear(y, xh, c, z, xl), linear(*to)))
    return lax.ppermute(value, AXES, pairs[::-1] if turned else pairs)


def along_z(value, by):
    return move(value, lambda y, xh, c, z, xl: (y, xh, c, z + by, xl))


def along_y(value, by, turned=False):
    return move(value, lambda y, xh, c, z, xl: (y + by, xh, c, z, xl), turned)


def other_xl(value):
    return move(value, lambda y, xh, c, z, xl: (y, xh, c, z, xl + 1))


def other_xh(value):
    return move(value, lambda y, xh, c, z, xl: (y, xh + 1, c, z, xl))


def other_core(value):
    return move(value, lambda y, xh, c, z, xl: (y, xh, c + 1, z, xl))


def products_kernel(units, n_shards, width, *refs):
    sources, out = refs[: 2 * n_shards], refs[2 * n_shards]
    held, full, arrived = refs[2 * n_shards + 1 :]
    core = lax.rem(lax.axis_index("tok"), NC)
    n_rows = width // (NY * NXH)
    depth = held.shape[2]
    half = depth // 2
    copies = []
    for i in range(n_shards):
        for side in range(2):
            place = held.at[i, :, side * half : (side + 1) * half]
            copies.append(pltpu.make_async_copy(sources[2 * i + side], place, arrived.at[i, side]))
            copies[-1].start()
    peak = jnp.zeros((16, depth), jnp.float32)
    for i in range(n_shards):
        copies[2 * i].wait()
        copies[2 * i + 1].wait()
        rows = jnp.max(jnp.abs(held[i]).reshape(width // 16, 16, depth), axis=0)
        peak = jnp.maximum(peak, rows.astype(jnp.float32))
    peak = jnp.maximum(jnp.max(peak), 1e-18)

    for c in range(NC):

        @pl.when(core == c)
        def _():
            for slot, (a, b) in enumerate(units[c]):
                full[:width, slot * width : (slot + 1) * width] = lax.dot_general(
                    held[a], held[b], (((1,), (1,)), ((), ())), preferred_element_type=jnp.float32
                )

    column = lax.broadcasted_iota(jnp.int32, (1, full.shape[1]), 1)
    fraction = lax.rem(column * 7, 16).astype(jnp.float32) * 0.0625
    exponent = jnp.ceil(2.0 * jnp.log2(jnp.full((1, full.shape[1]), peak))) + (depth.bit_length() - 15) + fraction
    exponents = jnp.broadcast_to(jnp.maximum(exponent, -125.0), (out.shape[2] - n_rows, full.shape[1]))
    for k in range(NY * NXH):
        out[k // NXH, k % NXH, :n_rows, :] = full[k * n_rows : (k + 1) * n_rows, :]
        out[k // NXH, k % NXH, n_rows:, :] = exponents


def products(units, shards):
    width, half = shards[0][0].shape
    n_units = len(units[0])
    padded = -(-(width // (NY * NXH)) // 8) * 8
    flat = [side for shard in shards for side in shard]
    return pl.pallas_call(
        functools.partial(products_kernel, units, len(shards), width),
        out_shape=jax.ShapeDtypeStruct((NY, NXH, padded, n_units * width), jnp.float32),
        in_specs=[pl.BlockSpec(memory_space=pl.ANY)] * len(flat),
        out_specs=pl.BlockSpec(memory_space=pltpu.VMEM),
        scratch_shapes=[
            pltpu.VMEM((len(shards), width, 2 * half), shards[0][0].dtype),
            pltpu.VMEM((width, n_units * width), jnp.float32),
            pltpu.SemaphoreType.DMA((len(shards), 2)),
        ],
        compiler_params=pltpu.CompilerParams(vmem_limit_bytes=20 * 1024 * 1024),
        cost_estimate=pl.CostEstimate(
            flops=n_units * 4 * width * width * half, bytes_accessed=8 * 1024 * 1024, transcendentals=0
        ),
    )(*flat)


def at_exponent(value, n_rows):
    return lax.broadcasted_iota(jnp.int32, value.shape, value.ndim - 2) == n_rows


def exponent_row(value, n_rows):
    return lax.slice_in_dim(value, n_rows, n_rows + 1, axis=value.ndim - 2)


def packed(value, n_rows):
    scaled = value * jnp.exp2(-exponent_row(value, n_rows))
    return jnp.where(at_exponent(value, n_rows), value, scaled).astype(jnp.float16)


def unpacked(value, n_rows):
    value = value.astype(jnp.float32)
    return jnp.where(at_exponent(value, n_rows), value, value * jnp.exp2(exponent_row(value, n_rows)))


def added(a, b, n_rows):
    return jnp.where(at_exponent(a, n_rows), jnp.maximum(a, b) + 1.3125, a + b)


def tied(value, *others):
    return lax.optimization_barrier((value, *others))[0]


def chunk_of(part, at):
    return lax.dynamic_index_in_dim(part, lax.rem(at, part.shape[0]), 0, keepdims=False)


def y_first(part, n_rows, y_at):
    far = chunk_of(part, y_at + 2)
    return packed(far[0], n_rows), packed(far[1], n_rows)


def y_second(part, arrived, n_rows, y_at):
    above, below = chunk_of(part, y_at + 1), chunk_of(part, y_at + 3)
    first = added(above[0], unpacked(arrived[0], n_rows), n_rows)
    second = added(below[1], unpacked(arrived[1], n_rows), n_rows)
    to_above = packed(jnp.stack([first, above[1]]), n_rows)
    to_below = packed(jnp.stack([below[0], second]), n_rows)
    return to_above, to_below


def y_last(part, arrived, n_rows, y_at):
    summed = added(unpacked(arrived[0], n_rows), unpacked(arrived[1], n_rows), n_rows)
    return added(chunk_of(part, y_at), summed, n_rows)


def x_give(summed, n_rows, xh_at):
    return packed(chunk_of(summed, xh_at + 1), n_rows)


def x_last(summed, arrived, n_rows, xh_at):
    return added(chunk_of(summed, xh_at), unpacked(arrived, n_rows), n_rows)


HELD = (
    ((1, 0), (-1, 1), (1, 1), (3, 0), (0, 0), (3, 1), (4, 0), (4, 1)),
    ((2, 0), (-1, 0), (-2, 0), (-3, 0), (0, 1), (2, 1), (-2, 1), (-3, 1)),
)


def assemble_kernel(width, count, mine, theirs, previous, out, stack):
    n_rows = previous.shape[0]
    core = lax.rem(lax.axis_index("tok"), NC)
    feat = lax.axis_index("feat")
    z_at, xl_at = feat // NXL, lax.rem(feat, NXL)
    for c in range(NC):

        @pl.when(core == c)
        def _():
            for slot in range(len(HELD[c])):
                columns = slice(slot * width, (slot + 1) * width)
                dz, dx = HELD[c][slot]
                stack[dz % NZ * NXL + dx, :n_rows, :] = mine[c * n_rows : (c + 1) * n_rows, columns]
                dz, dx = HELD[1 - c][slot]
                stack[dz % NZ * NXL + dx, :n_rows, :] = theirs[:, columns]

    for f in range(N_FEAT):
        at = lax.rem(f // NXL - z_at + NZ, NZ) * NXL + lax.rem(f % NXL + xl_at, NXL)
        columns = slice(f * width, (f + 1) * width)
        cov = stack[at, :n_rows, :] * (1.0 / count)
        out[:, columns] = (PRIOR * previous[:, columns] + cov) * (1.0 / (PRIOR + 1))


def assemble(mine, theirs, previous, width, count):
    n_rows = previous.shape[0]
    return pl.pallas_call(
        functools.partial(assemble_kernel, width, count),
        out_shape=jax.ShapeDtypeStruct(previous.shape, jnp.float32),
        in_specs=[pl.BlockSpec(memory_space=pltpu.VMEM)] * 3,
        out_specs=pl.BlockSpec(memory_space=pltpu.VMEM),
        scratch_shapes=[pltpu.VMEM((N_FEAT, -(-n_rows // 8) * 8, width), jnp.float32)],
        compiler_params=pltpu.CompilerParams(vmem_limit_bytes=14 * 1024 * 1024),
        cost_estimate=pl.CostEstimate(flops=0, bytes_accessed=4 * 1024 * 1024, transcendentals=0),
    )(mine, theirs, previous)


def per_device(gradients, previous):
    width = gradients.shape[1]
    count = gradients.shape[0] * N_TOK
    n_rows = previous.shape[0]
    tok = lax.axis_index("tok")
    y_at, xh_at, c_at = tok // (NXH * NC), lax.rem(tok // NC, NXH), lax.rem(tok, NC)

    own = gradients.T
    after, before, across = along_z(own, -1), along_z(own, 1), other_xl(own)
    own_2 = other_core(own)
    after2, before2 = along_z(after, -1), along_z(before, 1)
    across2 = other_xl(after2)
    after_2, before_2, across_2 = (other_core(tied(shard, own_2)) for shard in (after, before, across))
    after2_2 = other_core(after2)

    near = [(own, own_2), (after, after_2), (before, before_2), (across, across_2), (after2, after2_2)]
    rows = n_rows * NC
    part1 = products(
        (((0, 1), (3, 2), (2, 3), (2, 4), (0, 0)), ((0, 4), (1, 0), (4, 0), (4, 2), (0, 3))), near
    )
    far1 = y_first(part1, rows, y_at)
    half1 = along_y(far1[0], 1), along_y(far1[1], -1)
    across2_2, before2_2 = other_core(tied(across2, *far1)), other_core(tied(before2, *far1))

    far = [(own, own_2), (before, before_2), (before2, before2_2), (across2, across2_2), (after2, after2_2)]
    part2 = products((((1, 3), (2, 4), (2, 3)), ((0, 3), (3, 0), (3, 1))), far)
    far2 = y_first(part2, rows, y_at)
    half2 = along_y(far2[0], 1, True), along_y(far2[1], -1, True)
    half1 = lax.optimization_barrier(half1)
    give1 = y_second(part1, half1, rows, y_at)
    got1 = lax.optimization_barrier((along_y(give1[0], 1), along_y(give1[1], -1)))
    half2 = lax.optimization_barrier((*half2, *give1))[:2]
    give2 = y_second(part2, half2, rows, y_at)
    got2 = lax.optimization_barrier((along_y(give2[0], 1, True), along_y(give2[1], -1, True)))
    summed1 = y_last(part1, got1, rows, y_at)
    x_got1 = other_xh(x_give(summed1, rows, xh_at))
    sum1 = x_last(summed1, x_got1, rows, xh_at)

    def shifted(value, low, high, xh_by=0):
        def where(y, xh, c, z, xl):
            by = (low, high)[c]
            return None if by is None else (y, xh + xh_by, c, z + by[0], xl + by[1])

        return move(value, where)

    w = width
    got_a = shifted(sum1[:, w : 2 * w], (0, 1), (1, 0))
    summed2 = y_last(part2, got2, rows, y_at)
    keep, give = chunk_of(summed2, xh_at), packed(chunk_of(summed2, xh_at + 1), rows)
    kept = packed(keep, rows)
    joined = jnp.concatenate([packed(sum1[:, 2 * w : 4 * w], rows), kept[:, :w]], axis=1)
    joined = shifted(joined, (-1, 0), (2, 0))
    d_other = shifted(give[:, :w], (-1, 0), (0, 0), 1)
    e_same, e_other = shifted(kept[:, w:], (-2, 0), (2, 1)), shifted(give[:, w:], (-2, 0), (2, 1), 1)
    joined, d_other, e_same, e_other = lax.optimization_barrier((joined, d_other, e_same, e_other))
    got_b, d_same = unpacked(joined[:, : 2 * w], rows), joined[:, 2 * w :]
    got_d = jnp.where(c_at == 0, unpacked(d_same, rows), keep[:, :w]) + unpacked(d_other, rows)
    got_e = unpacked(e_same, rows) + unpacked(e_other, rows)
    mine = jnp.concatenate([sum1[:, :w], got_a, got_b, sum1[:, 4 * w :], got_d, got_e], axis=1)
    theirs = other_core(lax.dynamic_slice_in_dim(mine, (1 - c_at) * n_rows, n_rows, 0))
    return assemble(mine, theirs, previous, width, count)


def solution(mesh):
    placed = (P("tok", "feat"), P(("feat", "tok"), None))
    return jax.shard_map(
        per_device, mesh=mesh, in_specs=placed, out_specs=P(("feat", "tok"), None), check_vma=False
    )
```

```python
import functools

import jax
import jax.numpy as jnp
from jax import lax
from jax.experimental import pallas as pl
from jax.experimental.pallas import tpu as pltpu
from jax.sharding import PartitionSpec as P

PRIOR = 1
AXES = ("tok", "feat")
NY, NXH, NC, NZ, NXL = 4, 2, 2, 8, 2
N_TOK, N_FEAT = NY * NXH * NC, NZ * NXL


def linear(y, xh, c, z, xl):
    return ((y % NY * NXH + xh % NXH) * NC + c % NC) * N_FEAT + z % NZ * NXL + xl % NXL


def move(value, where, turned=False):
    pairs = []
    for y in range(NY):
        for xh in range(NXH):
            for c in range(NC):
                for z in range(NZ):
                    for xl in range(NXL):
                        to = where(y, xh, c, z, xl)
                        if to is not None:
                            pairs.append((linear(y, xh, c, z, xl), linear(*to)))
    return lax.ppermute(value, AXES, pairs[::-1] if turned else pairs)


def along_z(value, by):
    return move(value, lambda y, xh, c, z, xl: (y, xh, c, z + by, xl))


def along_y(value, by, turned=False):
    return move(value, lambda y, xh, c, z, xl: (y + by, xh, c, z, xl), turned)


def other_xl(value):
    return move(value, lambda y, xh, c, z, xl: (y, xh, c, z, xl + 1))


def other_xh(value):
    return move(value, lambda y, xh, c, z, xl: (y, xh + 1, c, z, xl))


def other_core(value):
    return move(value, lambda y, xh, c, z, xl: (y, xh, c + 1, z, xl))


def products_kernel(units, n_shards, width, *refs):
    sources, out = refs[: 2 * n_shards], refs[2 * n_shards]
    held, full, arrived = refs[2 * n_shards + 1 :]
    core = lax.rem(lax.axis_index("tok"), NC)
    n_rows = width // (NY * NXH)
    depth = held.shape[2]
    half = depth // 2
    copies = []
    for i in range(n_shards):
        for side in range(2):
            place = held.at[i, :, side * half : (side + 1) * half]
            copies.append(pltpu.make_async_copy(sources[2 * i + side], place, arrived.at[i, side]))
            copies[-1].start()
    peak = jnp.zeros((16, depth), jnp.float32)
    for i in range(n_shards):
        copies[2 * i].wait()
        copies[2 * i + 1].wait()
        rows = jnp.max(jnp.abs(held[i]).reshape(width // 16, 16, depth), axis=0)
        peak = jnp.maximum(peak, rows.astype(jnp.float32))
    peak = jnp.maximum(jnp.max(peak), 1e-18)

    for c in range(NC):

        @pl.when(core == c)
        def _():
            for slot, (a, b) in enumerate(units[c]):
                full[:width, slot * width : (slot + 1) * width] = lax.dot_general(
                    held[a], held[b], (((1,), (1,)), ((), ())), preferred_element_type=jnp.float32
                )

    column = lax.broadcasted_iota(jnp.int32, (1, full.shape[1]), 1)
    fraction = lax.rem(column * 7, 16).astype(jnp.float32) * 0.0625
    exponent = jnp.ceil(2.0 * jnp.log2(jnp.full((1, full.shape[1]), peak))) + (depth.bit_length() - 15) + fraction
    exponents = jnp.broadcast_to(jnp.maximum(exponent, -125.0), (out.shape[2] - n_rows, full.shape[1]))
    for k in range(NY * NXH):
        out[k // NXH, k % NXH, :n_rows, :] = full[k * n_rows : (k + 1) * n_rows, :]
        out[k // NXH, k % NXH, n_rows:, :] = exponents


def products(units, shards):
    width, half = shards[0][0].shape
    n_units = len(units[0])
    padded = -(-(width // (NY * NXH)) // 8) * 8
    flat = [side for shard in shards for side in shard]
    return pl.pallas_call(
        functools.partial(products_kernel, units, len(shards), width),
        out_shape=jax.ShapeDtypeStruct((NY, NXH, padded, n_units * width), jnp.float32),
        in_specs=[pl.BlockSpec(memory_space=pl.ANY)] * len(flat),
        out_specs=pl.BlockSpec(memory_space=pltpu.VMEM),
        scratch_shapes=[
            pltpu.VMEM((len(shards), width, 2 * half), shards[0][0].dtype),
            pltpu.VMEM((width, n_units * width), jnp.float32),
            pltpu.SemaphoreType.DMA((len(shards), 2)),
        ],
        compiler_params=pltpu.CompilerParams(vmem_limit_bytes=20 * 1024 * 1024),
        cost_estimate=pl.CostEstimate(
            flops=n_units * 4 * width * width * half, bytes_accessed=8 * 1024 * 1024, transcendentals=0
        ),
    )(*flat)


def at_exponent(value, n_rows):
    return lax.broadcasted_iota(jnp.int32, value.shape, value.ndim - 2) == n_rows


def exponent_row(value, n_rows):
    return lax.slice_in_dim(value, n_rows, n_rows + 1, axis=value.ndim - 2)


def packed(value, n_rows):
    scaled = value * jnp.exp2(-exponent_row(value, n_rows))
    return jnp.where(at_exponent(value, n_rows), value, scaled).astype(jnp.float16)


def unpacked(value, n_rows):
    value = value.astype(jnp.float32)
    return jnp.where(at_exponent(value, n_rows), value, value * jnp.exp2(exponent_row(value, n_rows)))


def added(a, b, n_rows):
    return jnp.where(at_exponent(a, n_rows), jnp.maximum(a, b) + 1.3125, a + b)


def tied(value, *others):
    return lax.optimization_barrier((value, *others))[0]


def chunk_of(part, at):
    return lax.dynamic_index_in_dim(part, lax.rem(at, part.shape[0]), 0, keepdims=False)


def y_first(part, n_rows, y_at):
    far = chunk_of(part, y_at + 2)
    return packed(far[0], n_rows), packed(far[1], n_rows)


def y_second(part, arrived, n_rows, y_at):
    above, below = chunk_of(part, y_at + 1), chunk_of(part, y_at + 3)
    first = added(above[0], unpacked(arrived[0], n_rows), n_rows)
    second = added(below[1], unpacked(arrived[1], n_rows), n_rows)
    to_above = packed(jnp.stack([first, above[1]]), n_rows)
    to_below = packed(jnp.stack([below[0], second]), n_rows)
    return to_above, to_below


def y_last(part, arrived, n_rows, y_at):
    summed = added(unpacked(arrived[0], n_rows), unpacked(arrived[1], n_rows), n_rows)
    return added(chunk_of(part, y_at), summed, n_rows)


def x_give(summed, n_rows, xh_at):
    return packed(chunk_of(summed, xh_at + 1), n_rows)


def x_last(summed, arrived, n_rows, xh_at):
    return added(chunk_of(summed, xh_at), unpacked(arrived, n_rows), n_rows)


HELD = (
    ((1, 0), (-1, 1), (1, 1), (3, 0), (0, 0), (3, 1), (4, 0), (4, 1)),
    ((2, 0), (-1, 0), (-2, 0), (-3, 0), (0, 1), (2, 1), (-2, 1), (-3, 1)),
)


def assemble_kernel(width, count, mine, theirs, previous, out, stack):
    n_rows = previous.shape[0]
    core = lax.rem(lax.axis_index("tok"), NC)
    feat = lax.axis_index("feat")
    z_at, xl_at = feat // NXL, lax.rem(feat, NXL)
    for c in range(NC):

        @pl.when(core == c)
        def _():
            for slot in range(len(HELD[c])):
                columns = slice(slot * width, (slot + 1) * width)
                dz, dx = HELD[c][slot]
                stack[dz % NZ * NXL + dx, :n_rows, :] = mine[c * n_rows : (c + 1) * n_rows, columns]
                dz, dx = HELD[1 - c][slot]
                stack[dz % NZ * NXL + dx, :n_rows, :] = theirs[:, columns]

    for f in range(N_FEAT):
        at = lax.rem(f // NXL - z_at + NZ, NZ) * NXL + lax.rem(f % NXL + xl_at, NXL)
        columns = slice(f * width, (f + 1) * width)
        cov = stack[at, :n_rows, :] * (1.0 / count)
        out[:, columns] = (PRIOR * previous[:, columns] + cov) * (1.0 / (PRIOR + 1))


def assemble(mine, theirs, previous, width, count):
    n_rows = previous.shape[0]
    return pl.pallas_call(
        functools.partial(assemble_kernel, width, count),
        out_shape=jax.ShapeDtypeStruct(previous.shape, jnp.float32),
        in_specs=[pl.BlockSpec(memory_space=pltpu.VMEM)] * 3,
        out_specs=pl.BlockSpec(memory_space=pltpu.VMEM),
        scratch_shapes=[pltpu.VMEM((N_FEAT, -(-n_rows // 8) * 8, width), jnp.float32)],
        compiler_params=pltpu.CompilerParams(vmem_limit_bytes=14 * 1024 * 1024),
        cost_estimate=pl.CostEstimate(flops=0, bytes_accessed=4 * 1024 * 1024, transcendentals=0),
    )(mine, theirs, previous)


def per_device(gradients, previous):
    width = gradients.shape[1]
    count = gradients.shape[0] * N_TOK
    n_rows = previous.shape[0]
    tok = lax.axis_index("tok")
    y_at, xh_at, c_at = tok // (NXH * NC), lax.rem(tok // NC, NXH), lax.rem(tok, NC)

    own = gradients.T
    after, before, across = along_z(own, -1), along_z(own, 1), other_xl(own)
    own_2 = other_core(own)
    after2, before2 = along_z(after, -1), along_z(before, 1)
    across2 = other_xl(after2)
    after_2, before_2, across_2 = (other_core(tied(shard, own_2)) for shard in (after, before, across))
    after2_2 = other_core(after2)

    near = [(own, own_2), (after, after_2), (before, before_2), (across, across_2), (after2, after2_2)]
    rows = n_rows * NC
    part1 = products(
        (((0, 1), (3, 2), (2, 3), (2, 4), (0, 0)), ((0, 4), (1, 0), (4, 0), (4, 2), (0, 3))), near
    )
    far1 = y_first(part1, rows, y_at)
    half1 = along_y(far1[0], 1), along_y(far1[1], -1)
    across2_2 = other_core(tied(across2, *far1))
    before2_2 = other_core(tied(before2, *half1))

    far = [(own, own_2), (before, before_2), (before2, before2_2), (across2, across2_2), (after2, after2_2)]
    part2 = products((((1, 3), (2, 4), (2, 3)), ((0, 3), (3, 0), (3, 1))), far)
    far2 = y_first(part2, rows, y_at)
    half2 = along_y(far2[0], 1, True), along_y(far2[1], -1, True)
    half1 = lax.optimization_barrier(half1)
    give1 = y_second(part1, half1, rows, y_at)
    got1 = lax.optimization_barrier((along_y(give1[0], 1), along_y(give1[1], -1)))
    half2 = lax.optimization_barrier((*half2, *give1))[:2]
    give2 = y_second(part2, half2, rows, y_at)
    got2 = lax.optimization_barrier((along_y(give2[0], 1, True), along_y(give2[1], -1, True)))
    summed1 = y_last(part1, got1, rows, y_at)
    x_got1 = other_xh(x_give(summed1, rows, xh_at))
    sum1 = x_last(summed1, x_got1, rows, xh_at)

    def shifted(value, low, high, xh_by=0):
        def where(y, xh, c, z, xl):
            by = (low, high)[c]
            return None if by is None else (y, xh + xh_by, c, z + by[0], xl + by[1])

        return move(value, where)

    w = width
    got_a = shifted(sum1[:, w : 2 * w], (0, 1), (1, 0))
    summed2 = y_last(part2, got2, rows, y_at)
    keep, give = chunk_of(summed2, xh_at), packed(chunk_of(summed2, xh_at + 1), rows)
    kept = packed(keep, rows)
    joined = jnp.concatenate([packed(sum1[:, 2 * w : 4 * w], rows), kept[:, :w]], axis=1)
    joined = shifted(joined, (-1, 0), (2, 0))
    d_other = shifted(give[:, :w], (-1, 0), (0, 0), 1)
    e_same, e_other = shifted(kept[:, w:], (-2, 0), (2, 1)), shifted(give[:, w:], (-2, 0), (2, 1), 1)
    joined, d_other, e_same, e_other = lax.optimization_barrier((joined, d_other, e_same, e_other))
    got_b, d_same = unpacked(joined[:, : 2 * w], rows), joined[:, 2 * w :]
    got_d = jnp.where(c_at == 0, unpacked(d_same, rows), keep[:, :w]) + unpacked(d_other, rows)
    got_e = unpacked(e_same, rows) + unpacked(e_other, rows)
    mine = jnp.concatenate([sum1[:, :w], got_a, got_b, sum1[:, 4 * w :], got_d, got_e], axis=1)
    theirs = other_core(lax.dynamic_slice_in_dim(mine, (1 - c_at) * n_rows, n_rows, 0))
    return assemble(mine, theirs, previous, width, count)


def solution(mesh):
    placed = (P("tok", "feat"), P(("feat", "tok"), None))
    return jax.shard_map(
        per_device, mesh=mesh, in_specs=placed, out_specs=P(("feat", "tok"), None), check_vma=False
    )
```

```python
import functools

import jax
import jax.numpy as jnp
from jax import lax
from jax.experimental import pallas as pl
from jax.experimental.pallas import tpu as pltpu
from jax.sharding import PartitionSpec as P

PRIOR = 1
AXES = ("tok", "feat")
NY, NXH, NC, NZ, NXL = 4, 2, 2, 8, 2
N_TOK, N_FEAT = NY * NXH * NC, NZ * NXL


def linear(y, xh, c, z, xl):
    return ((y % NY * NXH + xh % NXH) * NC + c % NC) * N_FEAT + z % NZ * NXL + xl % NXL


def move(value, where, turned=False):
    pairs = []
    for y in range(NY):
        for xh in range(NXH):
            for c in range(NC):
                for z in range(NZ):
                    for xl in range(NXL):
                        to = where(y, xh, c, z, xl)
                        if to is not None:
                            pairs.append((linear(y, xh, c, z, xl), linear(*to)))
    return lax.ppermute(value, AXES, pairs[::-1] if turned else pairs)


def along_z(value, by):
    return move(value, lambda y, xh, c, z, xl: (y, xh, c, z + by, xl))


def along_y(value, by, turned=False):
    return move(value, lambda y, xh, c, z, xl: (y + by, xh, c, z, xl), turned)


def other_xl(value):
    return move(value, lambda y, xh, c, z, xl: (y, xh, c, z, xl + 1))


def other_xh(value):
    return move(value, lambda y, xh, c, z, xl: (y, xh + 1, c, z, xl))


def other_core(value):
    return move(value, lambda y, xh, c, z, xl: (y, xh, c + 1, z, xl))


def products_kernel(units, n_shards, width, *refs):
    sources, out = refs[: 2 * n_shards], refs[2 * n_shards]
    held, full, arrived = refs[2 * n_shards + 1 :]
    core = lax.rem(lax.axis_index("tok"), NC)
    n_rows = width // (NY * NXH)
    depth = held.shape[2]
    half = depth // 2
    copies = []
    for i in range(n_shards):
        for side in range(2):
            place = held.at[i, :, side * half : (side + 1) * half]
            copies.append(pltpu.make_async_copy(sources[2 * i + side], place, arrived.at[i, side]))
            copies[-1].start()
    peak = jnp.zeros((16, depth), jnp.float32)
    for i in range(n_shards):
        copies[2 * i].wait()
        copies[2 * i + 1].wait()
        rows = jnp.max(jnp.abs(held[i]).reshape(width // 16, 16, depth), axis=0)
        peak = jnp.maximum(peak, rows.astype(jnp.float32))
    peak = jnp.maximum(jnp.max(peak), 1e-18)

    for c in range(NC):

        @pl.when(core == c)
        def _():
            for slot, (a, b) in enumerate(units[c]):
                full[:width, slot * width : (slot + 1) * width] = lax.dot_general(
                    held[a], held[b], (((1,), (1,)), ((), ())), preferred_element_type=jnp.float32
                )

    column = lax.broadcasted_iota(jnp.int32, (1, full.shape[1]), 1)
    fraction = lax.rem(column * 7, 16).astype(jnp.float32) * 0.0625
    exponent = jnp.ceil(2.0 * jnp.log2(jnp.full((1, full.shape[1]), peak))) + (depth.bit_length() - 15) + fraction
    exponents = jnp.broadcast_to(jnp.maximum(exponent, -125.0), (out.shape[2] - n_rows, full.shape[1]))
    for k in range(NY * NXH):
        out[k // NXH, k % NXH, :n_rows, :] = full[k * n_rows : (k + 1) * n_rows, :]
        out[k // NXH, k % NXH, n_rows:, :] = exponents


def products(units, shards):
    width, half = shards[0][0].shape
    n_units = len(units[0])
    padded = -(-(width // (NY * NXH)) // 8) * 8
    flat = [side for shard in shards for side in shard]
    return pl.pallas_call(
        functools.partial(products_kernel, units, len(shards), width),
        out_shape=jax.ShapeDtypeStruct((NY, NXH, padded, n_units * width), jnp.float32),
        in_specs=[pl.BlockSpec(memory_space=pl.ANY)] * len(flat),
        out_specs=pl.BlockSpec(memory_space=pltpu.VMEM),
        scratch_shapes=[
            pltpu.VMEM((len(shards), width, 2 * half), shards[0][0].dtype),
            pltpu.VMEM((width, n_units * width), jnp.float32),
            pltpu.SemaphoreType.DMA((len(shards), 2)),
        ],
        compiler_params=pltpu.CompilerParams(vmem_limit_bytes=20 * 1024 * 1024),
        cost_estimate=pl.CostEstimate(
            flops=n_units * 4 * width * width * half, bytes_accessed=8 * 1024 * 1024, transcendentals=0
        ),
    )(*flat)


def at_exponent(value, n_rows):
    return lax.broadcasted_iota(jnp.int32, value.shape, value.ndim - 2) == n_rows


def exponent_row(value, n_rows):
    return lax.slice_in_dim(value, n_rows, n_rows + 1, axis=value.ndim - 2)


def packed(value, n_rows, flat=False):
    scaled = value * jnp.exp2(-exponent_row(value, n_rows))
    scaled = jnp.where(at_exponent(value, n_rows), value, scaled)
    if flat:
        scaled = scaled.reshape(-1, value.shape[-1])
    return scaled.astype(jnp.float16)


def unpacked(value, n_rows):
    value = value.astype(jnp.float32)
    return jnp.where(at_exponent(value, n_rows), value, value * jnp.exp2(exponent_row(value, n_rows)))


def added(a, b, n_rows):
    return jnp.where(at_exponent(a, n_rows), jnp.maximum(a, b) + 1.3125, a + b)


def tied(value, *others):
    return lax.optimization_barrier((value, *others))[0]


def chunk_of(part, at):
    return lax.dynamic_index_in_dim(part, lax.rem(at, part.shape[0]), 0, keepdims=False)


def y_first(part, n_rows, y_at):
    far = chunk_of(part, y_at + 2)
    return packed(far[0], n_rows), packed(far[1], n_rows)


def y_second(part, arrived, n_rows, y_at):
    above, below = chunk_of(part, y_at + 1), chunk_of(part, y_at + 3)
    first = added(above[0], unpacked(arrived[0], n_rows), n_rows)
    second = added(below[1], unpacked(arrived[1], n_rows), n_rows)
    to_above = packed(jnp.stack([first, above[1]]), n_rows, True)
    to_below = packed(jnp.stack([below[0], second]), n_rows, True)
    return to_above, to_below


def y_last(part, arrived, n_rows, y_at):
    arrived = [value.astype(jnp.float32).reshape(NXH, -1, value.shape[1]) for value in arrived]
    summed = added(unpacked(arrived[0], n_rows), unpacked(arrived[1], n_rows), n_rows)
    return added(chunk_of(part, y_at), summed, n_rows)


def x_give(summed, n_rows, xh_at):
    return packed(chunk_of(summed, xh_at + 1), n_rows)


def x_last(summed, arrived, n_rows, xh_at):
    return added(chunk_of(summed, xh_at), unpacked(arrived, n_rows), n_rows)


HELD = (
    ((1, 0), (-1, 1), (1, 1), (3, 0), (0, 0), (3, 1), (4, 0), (4, 1)),
    ((2, 0), (-1, 0), (-2, 0), (-3, 0), (0, 1), (2, 1), (-2, 1), (-3, 1)),
)


def assemble_kernel(width, count, mine, theirs, previous, out, stack):
    n_rows = previous.shape[0]
    core = lax.rem(lax.axis_index("tok"), NC)
    feat = lax.axis_index("feat")
    z_at, xl_at = feat // NXL, lax.rem(feat, NXL)
    for c in range(NC):

        @pl.when(core == c)
        def _():
            for slot in range(len(HELD[c])):
                columns = slice(slot * width, (slot + 1) * width)
                dz, dx = HELD[c][slot]
                stack[dz % NZ * NXL + dx, :n_rows, :] = mine[c * n_rows : (c + 1) * n_rows, columns]
                dz, dx = HELD[1 - c][slot]
                stack[dz % NZ * NXL + dx, :n_rows, :] = theirs[:, columns]

    for f in range(N_FEAT):
        at = lax.rem(f // NXL - z_at + NZ, NZ) * NXL + lax.rem(f % NXL + xl_at, NXL)
        columns = slice(f * width, (f + 1) * width)
        cov = stack[at, :n_rows, :] * (1.0 / count)
        out[:, columns] = (PRIOR * previous[:, columns] + cov) * (1.0 / (PRIOR + 1))


def assemble(mine, theirs, previous, width, count):
    n_rows = previous.shape[0]
    return pl.pallas_call(
        functools.partial(assemble_kernel, width, count),
        out_shape=jax.ShapeDtypeStruct(previous.shape, jnp.float32),
        in_specs=[pl.BlockSpec(memory_space=pltpu.VMEM)] * 3,
        out_specs=pl.BlockSpec(memory_space=pltpu.VMEM),
        scratch_shapes=[pltpu.VMEM((N_FEAT, -(-n_rows // 8) * 8, width), jnp.float32)],
        compiler_params=pltpu.CompilerParams(vmem_limit_bytes=14 * 1024 * 1024),
        cost_estimate=pl.CostEstimate(flops=0, bytes_accessed=4 * 1024 * 1024, transcendentals=0),
    )(mine, theirs, previous)


def per_device(gradients, previous):
    width = gradients.shape[1]
    count = gradients.shape[0] * N_TOK
    n_rows = previous.shape[0]
    tok = lax.axis_index("tok")
    y_at, xh_at, c_at = tok // (NXH * NC), lax.rem(tok // NC, NXH), lax.rem(tok, NC)

    own = gradients.T
    after, before, across = along_z(own, -1), along_z(own, 1), other_xl(own)
    own_2 = other_core(own)
    after2, before2 = along_z(after, -1), along_z(before, 1)
    across2 = other_xl(after2)
    after_2, before_2, across_2 = (other_core(tied(shard, own_2)) for shard in (after, before, across))
    after2_2 = other_core(after2)

    near = [(own, own_2), (after, after_2), (before, before_2), (across, across_2), (after2, after2_2)]
    rows = n_rows * NC
    part1 = products(
        (((0, 1), (3, 2), (2, 3), (2, 4), (0, 0)), ((0, 4), (1, 0), (4, 0), (4, 2), (0, 3))), near
    )
    far1 = y_first(part1, rows, y_at)
    half1 = along_y(far1[0], 1), along_y(far1[1], -1)
    across2_2, before2_2 = other_core(tied(across2, *far1)), other_core(tied(before2, *far1))

    far = [(own, own_2), (before, before_2), (before2, before2_2), (across2, across2_2), (after2, after2_2)]
    part2 = products((((1, 3), (2, 4), (2, 3)), ((0, 3), (3, 0), (3, 1))), far)
    far2 = y_first(part2, rows, y_at)
    half2 = along_y(far2[0], 1, True), along_y(far2[1], -1, True)
    half1 = lax.optimization_barrier(half1)
    give1 = y_second(part1, half1, rows, y_at)
    got1 = lax.optimization_barrier((along_y(give1[0], 1), along_y(give1[1], -1)))
    half2 = lax.optimization_barrier((*half2, *give1))[:2]
    give2 = y_second(part2, half2, rows, y_at)
    got2 = lax.optimization_barrier((along_y(give2[0], 1, True), along_y(give2[1], -1, True)))
    summed1 = y_last(part1, got1, rows, y_at)
    x_got1 = other_xh(x_give(summed1, rows, xh_at))
    sum1 = x_last(summed1, x_got1, rows, xh_at)

    def shifted(value, low, high, xh_by=0):
        def where(y, xh, c, z, xl):
            by = (low, high)[c]
            return None if by is None else (y, xh + xh_by, c, z + by[0], xl + by[1])

        return move(value, where)

    w = width
    got_a = shifted(sum1[:, w : 2 * w], (0, 1), (1, 0))
    summed2 = y_last(part2, got2, rows, y_at)
    keep, give = chunk_of(summed2, xh_at), packed(chunk_of(summed2, xh_at + 1), rows)
    kept = packed(keep, rows)
    joined = jnp.concatenate([packed(sum1[:, 2 * w : 4 * w], rows), kept[:, :w]], axis=1)
    joined = shifted(joined, (-1, 0), (2, 0))
    d_other = shifted(give[:, :w], (-1, 0), (0, 0), 1)
    e_same, e_other = shifted(kept[:, w:], (-2, 0), (2, 1)), shifted(give[:, w:], (-2, 0), (2, 1), 1)
    joined, d_other, e_same, e_other = lax.optimization_barrier((joined, d_other, e_same, e_other))
    got_b, d_same = unpacked(joined[:, : 2 * w], rows), joined[:, 2 * w :]
    got_d = jnp.where(c_at == 0, unpacked(d_same, rows), keep[:, :w]) + unpacked(d_other, rows)
    got_e = unpacked(e_same, rows) + unpacked(e_other, rows)
    mine = jnp.concatenate([sum1[:, :w], got_a, got_b, sum1[:, 4 * w :], got_d, got_e], axis=1)
    theirs = other_core(lax.dynamic_slice_in_dim(mine, (1 - c_at) * n_rows, n_rows, 0))
    return assemble(mine, theirs, previous, width, count)


def solution(mesh):
    placed = (P("tok", "feat"), P(("feat", "tok"), None))
    return jax.shard_map(
        per_device, mesh=mesh, in_specs=placed, out_specs=P(("feat", "tok"), None), check_vma=False
    )
```
